512 devices in a mesh: span: 32 (over z, core), head: 16 (over y, x).
Axes of the slice: x: 4, y: 4, z: 16, core: 2. Of those that a mesh axis runs over, the one named last changes fastest.
Arguments:
- query_rows: bfloat16 [5120, 6144], P('span', 'head'), may hold values from -6 to 6
- key_rows: bfloat16 [5120, 6144], P('span', 'head'), may hold values from -6 to 6
- value_rows: bfloat16 [5120, 6144], P('span', 'head'), may hold values from -6 to 6
- block_mask: int32 [32, 32], P('span'), may hold values from 0 to 1, as said below
- noise_level: int32 [32], P('span'), may hold values from 0 to 15
- level_gain: float32 [16, 6144], P(None, 'head'), may hold values from 0.5 to 2
- out_weight: bfloat16 [6144, 6144], P('head', 'span'), may hold values from -0.625 to 0.625
Outputs:
- update_rows: bfloat16 [5120, 6144], P('span', 'head')
The draws below stay inside these ranges and needn't reach their ends.
Inputs may be any that keep to these rules, and one draw needn't show every extreme that they name: block_mask[i, i] is 1, block_mask[i, i - 1] is 1 for i > 0, and block_mask[i, j] is 0 for j > i; farther below the diagonal entries are 0 or 1.
All inputs are finite; a program needn't handle non-finite values.
Results may differ from the reference program's by a relative error of at most 0.02.
Values may be sent and summed in bfloat16 or wider, within the bound.
A program may use at most 64 MiB of HBM per device.

```python
import jax
import jax.numpy as jnp
from jax import lax

D = 6144
HEADS = 48
HD = 128
TOK_DEV = 160
LEVELS = 16
SPANS = 32
TOKENS = 5120
HH = 6144


def draw_query_rows(key, part):
    key = jax.random.fold_in(key, 1)
    drawn = jnp.clip(jax.random.normal(key, (TOKENS, HH), jnp.float32), -6.0, 6.0)
    return drawn.astype(jnp.bfloat16)


def draw_key_rows(key, part):
    key = jax.random.fold_in(key, 2)
    drawn = jnp.clip(jax.random.normal(key, (TOKENS, HH), jnp.float32), -6.0, 6.0)
    return drawn.astype(jnp.bfloat16)


def draw_block_mask(key, part):
    key = jax.random.fold_in(key, 3)
    row_ids = jnp.arange(SPANS)[:, None]
    col_ids = jnp.arange(SPANS)[None, :]
    coins = jax.random.randint(key, (SPANS, SPANS), 0, 4)
    below = jnp.where((col_ids < row_ids) & ((coins < 3) | (col_ids == row_ids - 1)), 1, 0)
    return jnp.where(col_ids == row_ids, 1, below).astype(jnp.int32)


def touch_ends(drawn, stream_key, least, top_value):
    spot = [jax.random.randint(jax.random.fold_in(stream_key, axis), (), 0, length) for axis, length in enumerate(drawn.shape)]
    longest = drawn.shape.index(max(drawn.shape))
    next_to = spot[:longest] + [(spot[longest] + 1) % drawn.shape[longest]] + spot[longest + 1:]
    return drawn.at[tuple(spot)].set(least).at[tuple(next_to)].set(top_value)


def with_spikes(values, own_key, source, target, blocks, factor):
    owner, partner = [(jnp.arange(values.shape[axis_at]) // (values.shape[axis_at] // blocks)).reshape([-1 if axis == axis_at else 1 for axis in range(values.ndim)]) for axis_at in (source, target)]
    chosen = jax.random.permutation(own_key, blocks)[partner]
    strong = (owner == chosen) | (owner == (partner + blocks // 2) % blocks)
    return jnp.where(strong, factor * values, values)


def level_of(key, dims, cuts, least, top_value):
    factor_of, own = 1.0, jax.random.fold_in(key, 6)
    for axis_at, parts in cuts:
        steps = jnp.exp(jax.random.uniform(jax.random.fold_in(own, axis_at), (parts,), jnp.float32, least / len(cuts), top_value / len(cuts)))
        factor_of = factor_of * jnp.repeat(steps, dims[axis_at] // parts).reshape([-1 if axis == axis_at else 1 for axis in range(len(dims))])
    return factor_of


def centred(stream_key, shape, width, most, shards=(), kind=jnp.bfloat16):
    loudness = level_of(stream_key, shape, shards, -0.22, 0.18) if shards else 1.0
    entries = jax.random.normal(stream_key, shape, jnp.float32) * width * loudness
    return jnp.minimum(jnp.maximum(entries, -most), most).astype(kind)


def gaussian_with(own_key, shape, scale, most, cuts, heavy, kind=jnp.bfloat16):
    values = scale * jax.random.normal(own_key, shape, jnp.float32)
    if cuts:
        values = values * level_of(own_key, shape, cuts, -0.22, 0.18)
    return jnp.clip(with_spikes(values, jax.random.fold_in(own_key, 3), *heavy), -most, most).astype(kind)


def setup_inputs(seed: int = 0) -> dict:
    key_list = jax.random.split(jax.random.key(seed), 8)
    query_rows = draw_query_rows(jax.random.fold_in(key_list[7], 71), 0)
    key_rows = draw_key_rows(jax.random.fold_in(key_list[7], 71), 0)
    value_rows = centred(key_list[2], (TOKENS, HH), 1.0, 6.0, ((0, 32), (1, 16)))
    block_mask = draw_block_mask(jax.random.fold_in(key_list[7], 71), 0)
    noise_level = touch_ends(jax.random.randint(key_list[4], (SPANS,), 0, LEVELS), jax.random.fold_in(key_list[4], 1), 0, LEVELS - 1).astype(jnp.int32)
    level_gain = jnp.clip(0.5 + 1.5 * jax.random.uniform(key_list[5], (LEVELS, D), jnp.float32) ** level_of(key_list[5], (LEVELS, D), ((1, 16),), -0.2, 0.2), 0.5, 2.0)
    out_weight = gaussian_with(key_list[6], (HH, D), (HH // 16) ** -0.5, 0.625, ((0, 16), (1, 32)), (0, 1, 32, 2.75))
    return dict(query_rows=query_rows, key_rows=key_rows, value_rows=value_rows, block_mask=block_mask, noise_level=noise_level, level_gain=level_gain, out_weight=out_weight)


def reference(query_rows, key_rows, value_rows, block_mask, noise_level, level_gain, out_weight):
    query_spans = query_rows.reshape(SPANS, TOK_DEV, HEADS, HD)
    key_heads = key_rows.reshape(TOKENS, HEADS, HD).astype(jnp.float32)
    value_heads = value_rows.reshape(TOKENS, HEADS, HD).astype(jnp.float32)
    key_span = (jnp.arange(TOKENS) // TOK_DEV).astype(jnp.int32)

    def one_span(span_index):
        query_block = lax.dynamic_index_in_dim(query_spans, span_index, 0, False).astype(jnp.float32)
        scores = jnp.einsum("thd,khd->htk", query_block, key_heads) * (HD ** -0.5)
        visible = block_mask[span_index][key_span] > 0
        scores = jnp.where(visible[None, None, :], scores, -1e30)
        row_max = jnp.max(scores, axis=2, keepdims=True)
        probs = jnp.where(visible[None, None, :], jnp.exp(scores - row_max), 0.0)
        row_total = jnp.sum(probs, axis=2)
        rounded = lax.optimization_barrier(probs.astype(jnp.bfloat16)).astype(jnp.float32)
        weighted = jnp.einsum("htk,khd->thd", rounded, value_heads)
        result = weighted / jnp.transpose(row_total)[:, :, None]
        return result.reshape(TOK_DEV, HH).astype(jnp.bfloat16)

    attended = lax.map(one_span, jnp.arange(SPANS, dtype=jnp.int32)).reshape(TOKENS, HH)
    projected = jnp.dot(attended, out_weight, preferred_element_type=jnp.float32)
    gains = level_gain[noise_level]
    gated = projected.reshape(SPANS, TOK_DEV, D) * gains[:, None, :]
    return gated.reshape(TOKENS, D).astype(jnp.bfloat16)
```

```python
import functools
import math

import jax
import jax.numpy as jnp
from jax import lax
from jax.experimental import pallas as pl
from jax.experimental.pallas import tpu as pltpu
from jax.sharding import PartitionSpec as P

MESH = pl.DeviceIdType.MESH
HD = 128
NZ = 16
NX = 4
ROWS = 160
HALF = ROWS // 2
WIDTH = 384
HEADS = WIDTH // HD
NEG = -1e30
SCORE_SCALE = math.log2(math.e) / math.sqrt(HD)
KEY, VALUE, WEIGHT = 0, 1, 2


def kernel(
    q_hbm, k_hbm, v_hbm, mask_ref, level_ref, gain_hbm, w_hbm, out_ref,
    q_ref, gain_ref, kbuf, vbuf, wall, row_max, row_sum, acc, att, part,
    tx1, rx1, tx2, rx2, tx3, rx3, mid,
    ring_s, ring_r, sib_s, sib_r, s1, r1, s2, r2, s3, r3, load,
):
    span = lax.axis_index("span")
    group = lax.axis_index("head")
    z, core = span // 2, span % 2
    y, x = group // NX, group % NX
    z_up = (lax.rem(z + 1, NZ) * 2 + core, group)
    z_down = (lax.rem(z + NZ - 1, NZ) * 2 + core, group)
    sibling = (z * 2 + 1 - core, group)
    toward = [z_up, z_down]

    def in_plane(axis, by):
        if axis == 0:
            return (span, y * NX + lax.rem(x + by, NX))
        return (span, lax.rem(y + by, NX) * NX + x)

    own = [(k_hbm, kbuf.at[pl.ds(0, ROWS)]), (v_hbm, vbuf.at[pl.ds(0, ROWS)]),
           (w_hbm, wall.at[0, core]), (q_hbm, q_ref), (gain_hbm, gain_ref)]
    loads = [pltpu.make_async_copy(src, dst, load.at[i]) for i, (src, dst) in enumerate(own)]
    for copy in loads:
        copy.start()

    barrier = pltpu.get_barrier_semaphore()
    peers = [z_up, z_down, sibling] + [in_plane(a, b) for a in (0, 1) for b in (1, 2, 3)]
    for peer in peers:
        pl.semaphore_signal(barrier, inc=1, device_id=peer, device_id_type=MESH)
    pl.semaphore_wait(barrier, len(peers))

    def chunk_base(way, dist):
        return pl.multiple_of(320 + (dist - 1) * 640 + way * 320, 160)

    def chunk(kind, way, dist, own_ring=True):
        if kind == WEIGHT:
            slot = dist if isinstance(dist, int) and dist == 0 else dist + way * 8
            return wall.at[slot, core if own_ring else 1 - core]
        buf = kbuf if kind == KEY else vbuf
        sub = 0 if own_ring else 1
        if isinstance(dist, int) and dist == 0:
            return buf.at[pl.ds(sub * ROWS, ROWS)]
        return buf.at[pl.ds(pl.multiple_of(chunk_base(way, dist) + sub * ROWS, 160), ROWS)]

    def ring_copy(kind, way, dist):
        return pltpu.make_async_remote_copy(
            src_ref=chunk(kind, way, dist),
            dst_ref=chunk(kind, way, dist + 1),
            send_sem=ring_s.at[kind, way, dist],
            recv_sem=ring_r.at[kind, way, dist + 1],
            device_id=toward[way],
            device_id_type=MESH,
        )

    def first_hop(kind, way):
        return pltpu.make_async_remote_copy(
            src_ref=own[kind][0],
            dst_ref=chunk(kind, way, 1),
            send_sem=ring_s.at[kind, way, 0],
            recv_sem=ring_r.at[kind, way, 1],
            device_id=toward[way],
            device_id_type=MESH,
        )

    def far_copy(kind, way):
        src, dst = chunk(kind, way, 7), chunk(kind, 0, 8)
        if kind == WEIGHT:
            src, dst = src.at[pl.ds(way * 96, 96)], dst.at[pl.ds(way * 96, 96)]
        return pltpu.make_async_remote_copy(
            src_ref=src,
            dst_ref=dst,
            send_sem=ring_s.at[kind, way, 7],
            recv_sem=ring_r.at[kind, way, 8],
            device_id=toward[way],
            device_id_type=MESH,
        )

    def arrival(kind, way, dist):
        landed = chunk(kind, way, dist)
        return pltpu.make_async_remote_copy(
            src_ref=landed,
            dst_ref=landed,
            send_sem=ring_s.at[kind, way, dist - 1],
            recv_sem=ring_r.at[kind, way, dist],
            device_id=toward[way],
            device_id_type=MESH,
        )

    def sibling_copy(kind, way, dist):
        dst = chunk(kind, way, dist, kind == WEIGHT)
        return pltpu.make_async_remote_copy(
            src_ref=chunk(kind, way, dist),
            dst_ref=dst,
            send_sem=sib_s.at[kind, way, dist],
            recv_sem=sib_r.at[kind, way, dist],
            device_id=sibling,
            device_id_type=MESH,
        )

    def sibling_arrival(kind, way, dist):
        landed = chunk(kind, way, dist, False)
        return pltpu.make_async_remote_copy(
            src_ref=landed,
            dst_ref=landed,
            send_sem=sib_s.at[kind, way, dist],
            recv_sem=sib_r.at[kind, way, dist],
            device_id=sibling,
            device_id_type=MESH,
        )

    for kind in (KEY, VALUE, WEIGHT):
        for way in (0, 1):
            first_hop(kind, way).start()
    for kind in (KEY, VALUE, WEIGHT):
        loads[kind].wait()
        sibling_copy(kind, 0, 0).start()
    loads[3].wait()
    loads[4].wait()

    row_max[...] = jnp.full_like(row_max, NEG)
    row_sum[...] = jnp.zeros_like(row_sum)
    acc[...] = jnp.zeros_like(acc)

    def visible(chip, which):
        return mask_ref[0, lax.rem(chip + 2 * NZ, NZ) * 2 + which]

    def attend(base, seen):
        count = len(seen) * ROWS
        lane_span = lax.broadcasted_iota(jnp.int32, (1, count), 1) // ROWS
        bias = jnp.zeros((1, count), jnp.float32)
        for place, flag in enumerate(seen):
            bias = jnp.where(lane_span == place, jnp.where(flag > 0, 0.0, NEG), bias)
        for head in range(HEADS):
            cols = slice(head * HD, (head + 1) * HD)
            scores = lax.dot_general(
                q_ref[:, cols], kbuf[pl.ds(base, count), cols], (((1,), (1,)), ((), ())),
                preferred_element_type=jnp.float32,
            )
            scores = scores * SCORE_SCALE + bias
            old_max = row_max[head][:, 0:1]
            new_max = jnp.maximum(old_max, jnp.max(scores, axis=1, keepdims=True))
            probs = jnp.exp2(scores - new_max)
            factor = jnp.exp2(old_max - new_max)
            total = row_sum[head][:, 0:1] * factor + jnp.sum(probs, axis=1, keepdims=True)
            row_max[head] = jnp.broadcast_to(new_max, (ROWS, HD))
            row_sum[head] = jnp.broadcast_to(total, (ROWS, HD))
            acc[head] = acc[head] * factor + jnp.dot(
                probs.astype(jnp.bfloat16), vbuf[pl.ds(base, count), cols],
                preferred_element_type=jnp.float32,
            )

    sibling_arrival(KEY, 0, 0).wait_recv()
    sibling_arrival(VALUE, 0, 0).wait_recv()
    attend(0, [visible(z, core), visible(z, 1 - core)])

    def hop(dist, _):
        for kind in (KEY, VALUE, WEIGHT):
            for way in (0, 1):
                arrival(kind, way, dist).wait_recv()

                @pl.when(dist < 7)
                def _():
                    ring_copy(kind, way, dist).start()

                if kind != WEIGHT:
                    send_far = way == kind

                    @pl.when(dist == 7)
                    def _():
                        if send_far:
                            far_copy(kind, way).start()
                else:

                    @pl.when(dist == 7)
                    def _():
                        far_copy(kind, way).start()

                sibling_copy(kind, way, dist).start()
        for kind in (KEY, VALUE):
            for way in (0, 1):
                sibling_arrival(kind, way, dist).wait_recv()
        attend(
            chunk_base(0, dist),
            [
                visible(z - dist, core), visible(z - dist, 1 - core),
                visible(z + dist, core), visible(z + dist, 1 - core),
            ],
        )
        return 0

    lax.fori_loop(1, 8, hop, 0)

    far_copy(KEY, 0).wait_recv()
    sibling_copy(KEY, 0, 8).start()
    far_copy(VALUE, 1).wait_recv()
    sibling_copy(VALUE, 0, 8).start()
    sibling_arrival(KEY, 0, 8).wait_recv()
    sibling_arrival(VALUE, 0, 8).wait_recv()
    attend(chunk_base(0, 8), [visible(z - 8, core), visible(z - 8, 1 - core)])
    for head in range(HEADS):
        att[:, head * HD:(head + 1) * HD] = (acc[head] / row_sum[head]).astype(jnp.bfloat16)

    for way in (0, 1):
        far_copy(WEIGHT, way).wait_recv()
    sibling_copy(WEIGHT, 0, 8).start()
    sibling_arrival(WEIGHT, 0, 0).wait_recv()

    def weights_in(dist, _):
        for way in (0, 1):
            sibling_arrival(WEIGHT, way, dist).wait_recv()
        return 0

    lax.fori_loop(1, 8, weights_in, 0)
    sibling_arrival(WEIGHT, 0, 8).wait_recv()

    def project(column, row):
        block = row * NX + column
        away = lax.rem(z - block + NZ, NZ)
        slot = jnp.where(away <= 8, away, 24 - away)
        part[block] = lax.dot_general(
            att[...], wall[slot].reshape(WIDTH, WIDTH), (((1,), (1,)), ((), ())),
            preferred_element_type=jnp.float32,
        )

    here = [x, y]

    def block_at(half, lead, other):
        return other * NX + lead if half == 0 else lead * NX + other

    def share(half, lead, by):
        other = lax.rem(here[1 - half] + by, NX)
        return part[block_at(half, lead, other), half * HALF:(half + 1) * HALF, :]

    def send(src, dst, ssem, rsem, axis, by):
        return pltpu.make_async_remote_copy(
            src_ref=src, dst_ref=dst, send_sem=ssem, recv_sem=rsem,
            device_id=in_plane(axis, by), device_id_type=MESH,
        )

    def first_copy(half, way, by):
        at = (half, way, by)
        return send(tx1.at[at], rx1.at[at], s1.at[at], r1.at[at], half, 1 + 2 * way)

    def second_copy(half, way, by):
        at = (half, way, by)
        return send(tx2.at[at], rx2.at[at], s2.at[at], r2.at[at], half, 1 + 2 * way)

    def third_copy(half, by):
        at = (half, by - 1)
        return send(tx3.at[at], rx3.at[at], s3.at[at], r3.at[at], 1 - half, by)

    far_places = ((1, 0), (2, 3))

    for by in range(NX):
        project(lax.rem(x + 2, NX), lax.rem(y + by, NX))
        if by != 2:
            project(lax.rem(x + by, NX), lax.rem(y + 2, NX))
    for place in (0, 1):
        for half in (0, 1):
            far = lax.rem(here[half] + 2, NX)
            for way in (0, 1):
                by = far_places[way][place]
                tx1[half, way, by] = share(half, far, by).astype(jnp.bfloat16)
                first_copy(half, way, by).start()
    for column in (0, 1, 3):
        for row in (0, 1, 3):
            project(lax.rem(x + column, NX), lax.rem(y + row, NX))

    def near(half, way):
        return lax.rem(here[half] + 1 + 2 * way, NX)

    for place in (0, 1):
        for half in (0, 1):
            for way in (0, 1):
                by = far_places[1 - way][place]
                tx2[half, way, by] = share(half, near(half, way), by).astype(jnp.bfloat16)
                second_copy(half, way, by).start()
    for place in (0, 1):
        for half in (0, 1):
            for way in (0, 1):
                by = far_places[way][place]
                first_copy(half, way, by).wait_recv()
                term = share(half, near(half, way), by) + rx1[half, way, by].astype(jnp.float32)
                tx2[half, way, by] = term.astype(jnp.bfloat16)
                second_copy(half, way, by).start()
    for by in (2, 1, 3, 0):
        for half in (0, 1):
            for way in (0, 1):
                second_copy(half, way, by).wait_recv()
            total = (
                share(half, here[half], by)
                + rx2[half, 0, by].astype(jnp.float32)
                + rx2[half, 1, by].astype(jnp.float32)
            )
            if by:
                tx3[half, by - 1] = total.astype(jnp.bfloat16)
                third_copy(half, by).start()
            else:
                mid[half] = total

    levels = gain_ref.shape[0]
    chosen = lax.broadcasted_iota(jnp.int32, (levels, 1), 0) == level_ref[0]
    gain_row = jnp.sum(jnp.where(chosen, gain_ref[...], 0.0), axis=0, keepdims=True)
    for half in (0, 1):
        total = mid[half]
        for by in (1, 3, 2):
            third_copy(half, by).wait_recv()
            total = total + rx3[half, by - 1].astype(jnp.float32)
        out_ref[half * HALF:(half + 1) * HALF, :] = (total * gain_row).astype(jnp.bfloat16)

    for kind in (KEY, VALUE, WEIGHT):
        sibling_copy(kind, 0, 0).wait_send()
        sibling_copy(kind, 0, 8).wait_send()
        for way in (0, 1):
            first_hop(kind, way).wait_send()
            if kind == WEIGHT or kind == way:
                far_copy(kind, way).wait_send()

    def left(dist, _):
        for kind in (KEY, VALUE, WEIGHT):
            for way in (0, 1):
                sibling_copy(kind, way, dist).wait_send()

                @pl.when(dist < 7)
                def _():
                    ring_copy(kind, way, dist).wait_send()

        return 0

    lax.fori_loop(1, 8, left, 0)
    for half in (0, 1):
        for way in (0, 1):
            for by in range(NX):
                if by in far_places[way]:
                    first_copy(half, way, by).wait_send()
                second_copy(half, way, by).wait_send()
        for by in (1, 2, 3):
            third_copy(half, by).wait_send()


def on_device(query_rows, key_rows, value_rows, block_mask, noise_level, level_gain, out_weight):
    vmem = pl.BlockSpec(memory_space=pltpu.VMEM)
    hbm = pl.BlockSpec(memory_space=pl.ANY)
    smem = pl.BlockSpec(memory_space=pltpu.SMEM)
    dma = pltpu.SemaphoreType.DMA
    tokens = 2 * NZ * ROWS

    def b16(*shape):
        return pltpu.VMEM(shape, jnp.bfloat16)

    def f32(*shape):
        return pltpu.VMEM(shape, jnp.float32)

    return pl.pallas_call(
        kernel,
        out_shape=jax.ShapeDtypeStruct((ROWS, WIDTH), jnp.bfloat16),
        in_specs=[hbm, hbm, hbm, smem, smem, hbm, hbm],
        out_specs=vmem,
        scratch_shapes=[
            b16(ROWS, WIDTH), f32(*level_gain.shape),
            b16(tokens, WIDTH), b16(tokens, WIDTH), b16(NZ, 2, 192, WIDTH),
            f32(HEADS, ROWS, HD), f32(HEADS, ROWS, HD), f32(HEADS, ROWS, HD),
            b16(ROWS, WIDTH), f32(NX * NX, ROWS, WIDTH),
            b16(2, 2, 4, HALF, WIDTH), b16(2, 2, 4, HALF, WIDTH),
            b16(2, 2, 4, HALF, WIDTH), b16(2, 2, 4, HALF, WIDTH),
            b16(2, 3, HALF, WIDTH), b16(2, 3, HALF, WIDTH),
            f32(2, HALF, WIDTH),
            dma((3, 2, 8)), dma((3, 2, 9)), dma((3, 2, 9)), dma((3, 2, 9)),
            dma((2, 2, 4)), dma((2, 2, 4)), dma((2, 2, 4)), dma((2, 2, 4)), dma((2, 3)), dma((2, 3)),
            dma((5,)),
        ],
        compiler_params=pltpu.CompilerParams(
            collective_id=0, has_side_effects=True, vmem_limit_bytes=62 << 20
        ),
    )(query_rows, key_rows, value_rows, block_mask, noise_level, level_gain, out_weight.T)


def solution(mesh):
    return jax.shard_map(
        on_device,
        mesh=mesh,
        in_specs=(
            P("span", "head"),
            P("span", "head"),
            P("span", "head"),
            P("span", None),
            P("span"),
            P(None, "head"),
            P("head", "span"),
        ),
        out_specs=P("span", "head"),
        check_vma=False,
    )
```

```python
import functools
import math

import jax
import jax.numpy as jnp
from jax import lax
from jax.experimental import pallas as pl
from jax.experimental.pallas import tpu as pltpu
from jax.sharding import PartitionSpec as P

MESH = pl.DeviceIdType.MESH
HD = 128
NZ = 16
NX = 4
ROWS = 160
HALF = ROWS // 2
WIDTH = 384
HEADS = WIDTH // HD
NEG = -1e30
SCORE_SCALE = math.log2(math.e) / math.sqrt(HD)
KEY, VALUE, WEIGHT = 0, 1, 2


def kernel(
    q_hbm, k_hbm, v_hbm, mask_ref, level_ref, gain_hbm, w_hbm, out_ref,
    q_ref, gain_ref, kbuf, vbuf, wall, row_max, row_sum, acc, att, part,
    tx1, rx1, tx2, rx2, tx3, rx3, mid,
    ring_s, ring_r, sib_s, sib_r, s1, r1, s2, r2, s3, r3, load,
):
    span = lax.axis_index("span")
    group = lax.axis_index("head")
    z, core = span // 2, span % 2
    y, x = group // NX, group % NX
    z_up = (lax.rem(z + 1, NZ) * 2 + core, group)
    z_down = (lax.rem(z + NZ - 1, NZ) * 2 + core, group)
    sibling = (z * 2 + 1 - core, group)
    toward = [z_up, z_down]

    def in_plane(axis, by):
        if axis == 0:
            return (span, y * NX + lax.rem(x + by, NX))
        return (span, lax.rem(y + by, NX) * NX + x)

    own = [(k_hbm, kbuf.at[pl.ds(0, ROWS)]), (v_hbm, vbuf.at[pl.ds(0, ROWS)]),
           (w_hbm, wall.at[0, core]), (q_hbm, q_ref), (gain_hbm, gain_ref)]
    loads = [pltpu.make_async_copy(src, dst, load.at[i]) for i, (src, dst) in enumerate(own)]
    for copy in loads:
        copy.start()

    barrier = pltpu.get_barrier_semaphore()
    peers = [z_up, z_down, sibling] + [in_plane(a, b) for a in (0, 1) for b in (1, 2, 3)]
    for peer in peers:
        pl.semaphore_signal(barrier, inc=1, device_id=peer, device_id_type=MESH)
    pl.semaphore_wait(barrier, len(peers))

    def chunk_base(way, dist):
        return pl.multiple_of(320 + (dist - 1) * 640 + way * 320, 160)

    def chunk(kind, way, dist, own_ring=True):
        if kind == WEIGHT:
            slot = dist if isinstance(dist, int) and dist == 0 else dist + way * 8
            return wall.at[slot, core if own_ring else 1 - core]
        buf = kbuf if kind == KEY else vbuf
        sub = 0 if own_ring else 1
        if isinstance(dist, int) and dist == 0:
            return buf.at[pl.ds(sub * ROWS, ROWS)]
        return buf.at[pl.ds(pl.multiple_of(chunk_base(way, dist) + sub * ROWS, 160), ROWS)]

    def ring_copy(kind, way, dist):
        return pltpu.make_async_remote_copy(
            src_ref=chunk(kind, way, dist),
            dst_ref=chunk(kind, way, dist + 1),
            send_sem=ring_s.at[kind, way, dist],
            recv_sem=ring_r.at[kind, way, dist + 1],
            device_id=toward[way],
            device_id_type=MESH,
        )

    def first_hop(kind, way):
        return pltpu.make_async_remote_copy(
            src_ref=own[kind][0],
            dst_ref=chunk(kind, way, 1),
            send_sem=ring_s.at[kind, way, 0],
            recv_sem=ring_r.at[kind, way, 1],
            device_id=toward[way],
            device_id_type=MESH,
        )

    def far_copy(kind, way):
        src, dst = chunk(kind, way, 7), chunk(kind, 0, 8)
        if kind == WEIGHT:
            src, dst = src.at[pl.ds(way * 96, 96)], dst.at[pl.ds(way * 96, 96)]
        return pltpu.make_async_remote_copy(
            src_ref=src,
            dst_ref=dst,
            send_sem=ring_s.at[kind, way, 7],
            recv_sem=ring_r.at[kind, way, 8],
            device_id=toward[way],
            device_id_type=MESH,
        )

    def arrival(kind, way, dist):
        landed = chunk(kind, way, dist)
        return pltpu.make_async_remote_copy(
            src_ref=landed,
            dst_ref=landed,
            send_sem=ring_s.at[kind, way, dist - 1],
            recv_sem=ring_r.at[kind, way, dist],
            device_id=toward[way],
            device_id_type=MESH,
        )

    def sibling_copy(kind, way, dist):
        dst = chunk(kind, way, dist, kind == WEIGHT)
        return pltpu.make_async_remote_copy(
            src_ref=chunk(kind, way, dist),
            dst_ref=dst,
            send_sem=sib_s.at[kind, way, dist],
            recv_sem=sib_r.at[kind, way, dist],
            device_id=sibling,
            device_id_type=MESH,
        )

    def sibling_arrival(kind, way, dist):
        landed = chunk(kind, way, dist, False)
        return pltpu.make_async_remote_copy(
            src_ref=landed,
            dst_ref=landed,
            send_sem=sib_s.at[kind, way, dist],
            recv_sem=sib_r.at[kind, way, dist],
            device_id=sibling,
            device_id_type=MESH,
        )

    for kind in (KEY, VALUE, WEIGHT):
        for way in (0, 1):
            first_hop(kind, way).start()
    for kind in (KEY, VALUE, WEIGHT):
        loads[kind].wait()
        sibling_copy(kind, 0, 0).start()
    loads[3].wait()
    loads[4].wait()

    row_max[...] = jnp.full_like(row_max, NEG)
    row_sum[...] = jnp.zeros_like(row_sum)
    acc[...] = jnp.zeros_like(acc)

    def visible(chip, which):
        return mask_ref[0, lax.rem(chip + 2 * NZ, NZ) * 2 + which]

    def attend(base, seen):
        count = len(seen) * ROWS
        lane_span = lax.broadcasted_iota(jnp.int32, (1, count), 1) // ROWS
        bias = jnp.zeros((1, count), jnp.float32)
        for place, flag in enumerate(seen):
            bias = jnp.where(lane_span == place, jnp.where(flag > 0, 0.0, NEG), bias)
        for head in range(HEADS):
            cols = slice(head * HD, (head + 1) * HD)
            scores = lax.dot_general(
                q_ref[:, cols], kbuf[pl.ds(base, count), cols], (((1,), (1,)), ((), ())),
                preferred_element_type=jnp.float32,
            )
            scores = scores * SCORE_SCALE + bias
            old_max = row_max[head][:, 0:1]
            new_max = jnp.maximum(old_max, jnp.max(scores, axis=1, keepdims=True))
            probs = jnp.exp2(scores - new_max)
            factor = jnp.exp2(old_max - new_max)
            total = row_sum[head][:, 0:1] * factor + jnp.sum(probs, axis=1, keepdims=True)
            row_max[head] = jnp.broadcast_to(new_max, (ROWS, HD))
            row_sum[head] = jnp.broadcast_to(total, (ROWS, HD))
            acc[head] = acc[head] * factor + jnp.dot(
                probs.astype(jnp.bfloat16), vbuf[pl.ds(base, count), cols],
                preferred_element_type=jnp.float32,
            )

    sibling_arrival(KEY, 0, 0).wait_recv()
    sibling_arrival(VALUE, 0, 0).wait_recv()
    attend(0, [visible(z, core), visible(z, 1 - core)])

    def hop(dist, _):
        for kind in (KEY, VALUE):
            for way in (0, 1):
                arrival(kind, way, dist).wait_recv()

                @pl.when(dist < 7)
                def _():
                    ring_copy(kind, way, dist).start()

                if kind != WEIGHT:
                    send_far = way == kind

                    @pl.when(dist == 7)
                    def _():
                        if send_far:
                            far_copy(kind, way).start()
                else:

                    @pl.when(dist == 7)
                    def _():
                        far_copy(kind, way).start()

                sibling_copy(kind, way, dist).start()
        for kind in (KEY, VALUE):
            for way in (0, 1):
                sibling_arrival(kind, way, dist).wait_recv()
        attend(
            chunk_base(0, dist),
            [
                visible(z - dist, core), visible(z - dist, 1 - core),
                visible(z + dist, core), visible(z + dist, 1 - core),
            ],
        )
        for kind in (WEIGHT,):
            for way in (0, 1):
                arrival(kind, way, dist).wait_recv()

                @pl.when(dist < 7)
                def _():
                    ring_copy(kind, way, dist).start()

                if kind != WEIGHT:
                    send_far = way == kind

                    @pl.when(dist == 7)
                    def _():
                        if send_far:
                            far_copy(kind, way).start()
                else:

                    @pl.when(dist == 7)
                    def _():
                        far_copy(kind, way).start()

                sibling_copy(kind, way, dist).start()
        return 0

    lax.fori_loop(1, 8, hop, 0)

    far_copy(KEY, 0).wait_recv()
    sibling_copy(KEY, 0, 8).start()
    far_copy(VALUE, 1).wait_recv()
    sibling_copy(VALUE, 0, 8).start()
    sibling_arrival(KEY, 0, 8).wait_recv()
    sibling_arrival(VALUE, 0, 8).wait_recv()
    attend(chunk_base(0, 8), [visible(z - 8, core), visible(z - 8, 1 - core)])
    for head in range(HEADS):
        att[:, head * HD:(head + 1) * HD] = (acc[head] / row_sum[head]).astype(jnp.bfloat16)

    for way in (0, 1):
        far_copy(WEIGHT, way).wait_recv()
    sibling_copy(WEIGHT, 0, 8).start()
    sibling_arrival(WEIGHT, 0, 0).wait_recv()

    def weights_in(dist, _):
        for way in (0, 1):
            sibling_arrival(WEIGHT, way, dist).wait_recv()
        return 0

    lax.fori_loop(1, 8, weights_in, 0)
    sibling_arrival(WEIGHT, 0, 8).wait_recv()

    def project(column, row):
        block = row * NX + column
        away = lax.rem(z - block + NZ, NZ)
        slot = jnp.where(away <= 8, away, 24 - away)
        part[block] = lax.dot_general(
            att[...], wall[slot].reshape(WIDTH, WIDTH), (((1,), (1,)), ((), ())),
            preferred_element_type=jnp.float32,
        )

    here = [x, y]

    def block_at(half, lead, other):
        return other * NX + lead if half == 0 else lead * NX + other

    def share(half, lead, by):
        other = lax.rem(here[1 - half] + by, NX)
        return part[block_at(half, lead, other), half * HALF:(half + 1) * HALF, :]

    def send(src, dst, ssem, rsem, axis, by):
        return pltpu.make_async_remote_copy(
            src_ref=src, dst_ref=dst, send_sem=ssem, recv_sem=rsem,
            device_id=in_plane(axis, by), device_id_type=MESH,
        )

    def first_copy(half, way, by):
        at = (half, way, by)
        return send(tx1.at[at], rx1.at[at], s1.at[at], r1.at[at], half, 1 + 2 * way)

    def second_copy(half, way, by):
        at = (half, way, by)
        return send(tx2.at[at], rx2.at[at], s2.at[at], r2.at[at], half, 1 + 2 * way)

    def third_copy(half, by):
        at = (half, by - 1)
        return send(tx3.at[at], rx3.at[at], s3.at[at], r3.at[at], 1 - half, by)

    far_places = ((1, 0), (2, 3))
    near_order = ((2, 1, 3, 0), (1, 2, 3, 0))
    projected = set()

    def need(column, row):
        if (column, row) not in projected:
            projected.add((column, row))
            project(lax.rem(x + column, NX), lax.rem(y + row, NX))

    def need_share(half, lead_by, by):
        need(*((lead_by, by) if half == 0 else (by, lead_by)))

    for place in (0, 1):
        for half in (0, 1):
            far = lax.rem(here[half] + 2, NX)
            for way in (0, 1):
                by = far_places[way][place]
                need_share(half, 2, by)
                tx1[half, way, by] = share(half, far, by).astype(jnp.bfloat16)
                first_copy(half, way, by).start()

    def near(half, way):
        return lax.rem(here[half] + 1 + 2 * way, NX)

    for place in range(NX):
        for half in (0, 1):
            for way in (0, 1):
                by = near_order[way][place]
                need_share(half, 1 + 2 * way, by)
                term = share(half, near(half, way), by)
                if by in far_places[way]:
                    first_copy(half, way, by).wait_recv()
                    term = term + rx1[half, way, by].astype(jnp.float32)
                tx2[half, way, by] = term.astype(jnp.bfloat16)
                second_copy(half, way, by).start()
        if place == 0:
            for column in range(NX):
                for row in range(NX):
                    need(column, row)
    for by in (2, 1, 3, 0):
        for half in (0, 1):
            for way in (0, 1):
                second_copy(half, way, by).wait_recv()
            total = (
                share(half, here[half], by)
                + rx2[half, 0, by].astype(jnp.float32)
                + rx2[half, 1, by].astype(jnp.float32)
            )
            if by:
                tx3[half, by - 1] = total.astype(jnp.bfloat16)
                third_copy(half, by).start()
            else:
                mid[half] = total

    levels = gain_ref.shape[0]
    chosen = lax.broadcasted_iota(jnp.int32, (levels, 1), 0) == level_ref[0]
    gain_row = jnp.sum(jnp.where(chosen, gain_ref[...], 0.0), axis=0, keepdims=True)
    for half in (0, 1):
        total = mid[half]
        for by in (1, 3, 2):
            third_copy(half, by).wait_recv()
            total = total + rx3[half, by - 1].astype(jnp.float32)
        out_ref[half * HALF:(half + 1) * HALF, :] = (total * gain_row).astype(jnp.bfloat16)

    for kind in (KEY, VALUE, WEIGHT):
        sibling_copy(kind, 0, 0).wait_send()
        sibling_copy(kind, 0, 8).wait_send()
        for way in (0, 1):
            first_hop(kind, way).wait_send()
            if kind == WEIGHT or kind == way:
                far_copy(kind, way).wait_send()

    def left(dist, _):
        for kind in (KEY, VALUE, WEIGHT):
            for way in (0, 1):
                sibling_copy(kind, way, dist).wait_send()

                @pl.when(dist < 7)
                def _():
                    ring_copy(kind, way, dist).wait_send()

        return 0

    lax.fori_loop(1, 8, left, 0)
    for half in (0, 1):
        for way in (0, 1):
            for by in range(NX):
                if by in far_places[way]:
                    first_copy(half, way, by).wait_send()
                second_copy(half, way, by).wait_send()
        for by in (1, 2, 3):
            third_copy(half, by).wait_send()


def on_device(query_rows, key_rows, value_rows, block_mask, noise_level, level_gain, out_weight):
    vmem = pl.BlockSpec(memory_space=pltpu.VMEM)
    hbm = pl.BlockSpec(memory_space=pl.ANY)
    smem = pl.BlockSpec(memory_space=pltpu.SMEM)
    dma = pltpu.SemaphoreType.DMA
    tokens = 2 * NZ * ROWS

    def b16(*shape):
        return pltpu.VMEM(shape, jnp.bfloat16)

    def f32(*shape):
        return pltpu.VMEM(shape, jnp.float32)

    return pl.pallas_call(
        kernel,
        out_shape=jax.ShapeDtypeStruct((ROWS, WIDTH), jnp.bfloat16),
        in_specs=[hbm, hbm, hbm, smem, smem, hbm, hbm],
        out_specs=vmem,
        scratch_shapes=[
            b16(ROWS, WIDTH), f32(*level_gain.shape),
            b16(tokens, WIDTH), b16(tokens, WIDTH), b16(NZ, 2, 192, WIDTH),
            f32(HEADS, ROWS, HD), f32(HEADS, ROWS, HD), f32(HEADS, ROWS, HD),
            b16(ROWS, WIDTH), f32(NX * NX, ROWS, WIDTH),
            b16(2, 2, 4, HALF, WIDTH), b16(2, 2, 4, HALF, WIDTH),
            b16(2, 2, 4, HALF, WIDTH), b16(2, 2, 4, HALF, WIDTH),
            b16(2, 3, HALF, WIDTH), b16(2, 3, HALF, WIDTH),
            f32(2, HALF, WIDTH),
            dma((3, 2, 8)), dma((3, 2, 9)), dma((3, 2, 9)), dma((3, 2, 9)),
            dma((2, 2, 4)), dma((2, 2, 4)), dma((2, 2, 4)), dma((2, 2, 4)), dma((2, 3)), dma((2, 3)),
            dma((5,)),
        ],
        compiler_params=pltpu.CompilerParams(
            collective_id=0, has_side_effects=True, vmem_limit_bytes=62 << 20
        ),
    )(query_rows, key_rows, value_rows, block_mask, noise_level, level_gain, out_weight.T)


def solution(mesh):
    return jax.shard_map(
        on_device,
        mesh=mesh,
        in_specs=(
            P("span", "head"),
            P("span", "head"),
            P("span", "head"),
            P("span", None),
            P("span"),
            P(None, "head"),
            P("head", "span"),
        ),
        out_specs=P("span", "head"),
        check_vma=False,
    )
```

```python
import functools
import math

import jax
import jax.numpy as jnp
from jax import lax
from jax.experimental import pallas as pl
from jax.experimental.pallas import tpu as pltpu
from jax.sharding import PartitionSpec as P

MESH = pl.DeviceIdType.MESH
HD = 128
NZ = 16
NX = 4
ROWS = 160
HALF = ROWS // 2
WIDTH = 384
HEADS = WIDTH // HD
NEG = -1e30
SCORE_SCALE = math.log2(math.e) / math.sqrt(HD)
KEY, VALUE, WEIGHT = 0, 1, 2


def kernel(
    q_hbm, k_hbm, v_hbm, mask_ref, level_ref, gain_hbm, w_hbm, out_ref,
    q_ref, gain_ref, kbuf, vbuf, wall, row_max, row_sum, acc, att, part,
    tx1, rx1, tx2, rx2, tx3, rx3, mid,
    ring_s, ring_r, sib_s, sib_r, s1, r1, s2, r2, s3, r3, load,
):
    span = lax.axis_index("span")
    group = lax.axis_index("head")
    z, core = span // 2, span % 2
    y, x = group // NX, group % NX
    z_up = (lax.rem(z + 1, NZ) * 2 + core, group)
    z_down = (lax.rem(z + NZ - 1, NZ) * 2 + core, group)
    sibling = (z * 2 + 1 - core, group)
    toward = [z_up, z_down]

    def in_plane(axis, by):
        if axis == 0:
            return (span, y * NX + lax.rem(x + by, NX))
        return (span, lax.rem(y + by, NX) * NX + x)

    own = [(k_hbm, kbuf.at[pl.ds(0, ROWS)]), (v_hbm, vbuf.at[pl.ds(0, ROWS)]),
           (w_hbm, wall.at[0, core]), (q_hbm, q_ref), (gain_hbm, gain_ref)]
    loads = [pltpu.make_async_copy(src, dst, load.at[i]) for i, (src, dst) in enumerate(own)]
    for copy in loads:
        copy.start()

    barrier = pltpu.get_barrier_semaphore()
    peers = [z_up, z_down, sibling] + [in_plane(a, b) for a in (0, 1) for b in (1, 2, 3)]
    for peer in peers:
        pl.semaphore_signal(barrier, inc=1, device_id=peer, device_id_type=MESH)
    pl.semaphore_wait(barrier, len(peers))

    def chunk_base(way, dist):
        return pl.multiple_of(320 + (dist - 1) * 640 + way * 320, 160)

    def chunk(kind, way, dist, own_ring=True):
        if kind == WEIGHT:
            slot = dist if isinstance(dist, int) and dist == 0 else dist + way * 8
            return wall.at[slot, core if own_ring else 1 - core]
        buf = kbuf if kind == KEY else vbuf
        sub = 0 if own_ring else 1
        if isinstance(dist, int) and dist == 0:
            return buf.at[pl.ds(sub * ROWS, ROWS)]
        return buf.at[pl.ds(pl.multiple_of(chunk_base(way, dist) + sub * ROWS, 160), ROWS)]

    def ring_copy(kind, way, dist):
        return pltpu.make_async_remote_copy(
            src_ref=chunk(kind, way, dist),
            dst_ref=chunk(kind, way, dist + 1),
            send_sem=ring_s.at[kind, way, dist],
            recv_sem=ring_r.at[kind, way, dist + 1],
            device_id=toward[way],
            device_id_type=MESH,
        )

    def first_hop(kind, way):
        return pltpu.make_async_remote_copy(
            src_ref=own[kind][0],
            dst_ref=chunk(kind, way, 1),
            send_sem=ring_s.at[kind, way, 0],
            recv_sem=ring_r.at[kind, way, 1],
            device_id=toward[way],
            device_id_type=MESH,
        )

    def far_copy(kind, way):
        src, dst = chunk(kind, way, 7), chunk(kind, 0, 8)
        if kind == WEIGHT:
            src, dst = src.at[pl.ds(way * 96, 96)], dst.at[pl.ds(way * 96, 96)]
        return pltpu.make_async_remote_copy(
            src_ref=src,
            dst_ref=dst,
            send_sem=ring_s.at[kind, way, 7],
            recv_sem=ring_r.at[kind, way, 8],
            device_id=toward[way],
            device_id_type=MESH,
        )

    def arrival(kind, way, dist):
        landed = chunk(kind, way, dist)
        return pltpu.make_async_remote_copy(
            src_ref=landed,
            dst_ref=landed,
            send_sem=ring_s.at[kind, way, dist - 1],
            recv_sem=ring_r.at[kind, way, dist],
            device_id=toward[way],
            device_id_type=MESH,
        )

    def sibling_copy(kind, way, dist):
        dst = chunk(kind, way, dist, kind == WEIGHT)
        return pltpu.make_async_remote_copy(
            src_ref=chunk(kind, way, dist),
            dst_ref=dst,
            send_sem=sib_s.at[kind, way, dist],
            recv_sem=sib_r.at[kind, way, dist],
            device_id=sibling,
            device_id_type=MESH,
        )

    def sibling_arrival(kind, way, dist):
        landed = chunk(kind, way, dist, False)
        return pltpu.make_async_remote_copy(
            src_ref=landed,
            dst_ref=landed,
            send_sem=sib_s.at[kind, way, dist],
            recv_sem=sib_r.at[kind, way, dist],
            device_id=sibling,
            device_id_type=MESH,
        )

    for kind in (KEY, VALUE, WEIGHT):
        for way in (0, 1):
            first_hop(kind, way).start()
    for kind in (KEY, VALUE, WEIGHT):
        loads[kind].wait()
        sibling_copy(kind, 0, 0).start()
    loads[3].wait()
    loads[4].wait()

    row_max[...] = jnp.full_like(row_max, NEG)
    row_sum[...] = jnp.zeros_like(row_sum)
    acc[...] = jnp.zeros_like(acc)

    def visible(chip, which):
        return mask_ref[0, lax.rem(chip + 2 * NZ, NZ) * 2 + which]

    def attend(base, seen):
        count = len(seen) * ROWS
        lane_span = lax.broadcasted_iota(jnp.int32, (1, count), 1) // ROWS
        bias = jnp.zeros((1, count), jnp.float32)
        for place, flag in enumerate(seen):
            bias = jnp.where(lane_span == place, jnp.where(flag > 0, 0.0, NEG), bias)
        for head in range(HEADS):
            cols = slice(head * HD, (head + 1) * HD)
            scores = lax.dot_general(
                q_ref[:, cols], kbuf[pl.ds(base, count), cols], (((1,), (1,)), ((), ())),
                preferred_element_type=jnp.float32,
            )
            scores = scores * SCORE_SCALE + bias
            old_max = row_max[head][:, 0:1]
            new_max = jnp.maximum(old_max, jnp.max(scores, axis=1, keepdims=True))
            probs = jnp.exp2(scores - new_max)
            factor = jnp.exp2(old_max - new_max)
            total = row_sum[head][:, 0:1] * factor + jnp.sum(probs, axis=1, keepdims=True)
            row_max[head] = jnp.broadcast_to(new_max, (ROWS, HD))
            row_sum[head] = jnp.broadcast_to(total, (ROWS, HD))
            acc[head] = acc[head] * factor + jnp.dot(
                probs.astype(jnp.bfloat16), vbuf[pl.ds(base, count), cols],
                preferred_element_type=jnp.float32,
            )

    sibling_arrival(KEY, 0, 0).wait_recv()
    sibling_arrival(VALUE, 0, 0).wait_recv()
    attend(0, [visible(z, core), visible(z, 1 - core)])

    def hop(dist, _):
        for kind in (KEY, VALUE):
            for way in (0, 1):
                arrival(kind, way, dist).wait_recv()

                @pl.when(dist < 7)
                def _():
                    ring_copy(kind, way, dist).start()

                if kind != WEIGHT:
                    send_far = way == kind

                    @pl.when(dist == 7)
                    def _():
                        if send_far:
                            far_copy(kind, way).start()
                else:

                    @pl.when(dist == 7)
                    def _():
                        far_copy(kind, way).start()

                sibling_copy(kind, way, dist).start()
        for kind in (KEY, VALUE):
            for way in (0, 1):
                sibling_arrival(kind, way, dist).wait_recv()
        attend(
            chunk_base(0, dist),
            [
                visible(z - dist, core), visible(z - dist, 1 - core),
                visible(z + dist, core), visible(z + dist, 1 - core),
            ],
        )
        for kind in (WEIGHT,):
            for way in (0, 1):
                arrival(kind, way, dist).wait_recv()

                @pl.when(dist < 7)
                def _():
                    ring_copy(kind, way, dist).start()

                if kind != WEIGHT:
                    send_far = way == kind

                    @pl.when(dist == 7)
                    def _():
                        if send_far:
                            far_copy(kind, way).start()
                else:

                    @pl.when(dist == 7)
                    def _():
                        far_copy(kind, way).start()

                sibling_copy(kind, way, dist).start()
        return 0

    for dist in range(1, 8):
        hop(dist, 0)

    far_copy(KEY, 0).wait_recv()
    sibling_copy(KEY, 0, 8).start()
    far_copy(VALUE, 1).wait_recv()
    sibling_copy(VALUE, 0, 8).start()
    sibling_arrival(KEY, 0, 8).wait_recv()
    sibling_arrival(VALUE, 0, 8).wait_recv()
    attend(chunk_base(0, 8), [visible(z - 8, core), visible(z - 8, 1 - core)])
    for head in range(HEADS):
        att[:, head * HD:(head + 1) * HD] = (acc[head] / row_sum[head]).astype(jnp.bfloat16)

    for way in (0, 1):
        far_copy(WEIGHT, way).wait_recv()
    sibling_copy(WEIGHT, 0, 8).start()
    sibling_arrival(WEIGHT, 0, 0).wait_recv()

    def weights_in(dist, _):
        for way in (0, 1):
            sibling_arrival(WEIGHT, way, dist).wait_recv()
        return 0

    lax.fori_loop(1, 8, weights_in, 0)
    sibling_arrival(WEIGHT, 0, 8).wait_recv()

    def project(column, row):
        block = row * NX + column
        away = lax.rem(z - block + NZ, NZ)
        slot = jnp.where(away <= 8, away, 24 - away)
        part[block] = lax.dot_general(
            att[...], wall[slot].reshape(WIDTH, WIDTH), (((1,), (1,)), ((), ())),
            preferred_element_type=jnp.float32,
        )

    here = [x, y]

    def block_at(half, lead, other):
        return other * NX + lead if half == 0 else lead * NX + other

    def share(half, lead, by):
        other = lax.rem(here[1 - half] + by, NX)
        return part[block_at(half, lead, other), half * HALF:(half + 1) * HALF, :]

    def send(src, dst, ssem, rsem, axis, by):
        return pltpu.make_async_remote_copy(
            src_ref=src, dst_ref=dst, send_sem=ssem, recv_sem=rsem,
            device_id=in_plane(axis, by), device_id_type=MESH,
        )

    def first_copy(half, way, by):
        at = (half, way, by)
        return send(tx1.at[at], rx1.at[at], s1.at[at], r1.at[at], half, 1 + 2 * way)

    def second_copy(half, way, by):
        at = (half, way, by)
        return send(tx2.at[at], rx2.at[at], s2.at[at], r2.at[at], half, 1 + 2 * way)

    def third_copy(half, by):
        at = (half, by - 1)
        return send(tx3.at[at], rx3.at[at], s3.at[at], r3.at[at], 1 - half, by)

    far_places = ((1, 0), (2, 3))
    near_order = ((2, 1, 3, 0), (1, 2, 3, 0))
    projected = set()

    def need(column, row):
        if (column, row) not in projected:
            projected.add((column, row))
            project(lax.rem(x + column, NX), lax.rem(y + row, NX))

    def need_share(half, lead_by, by):
        need(*((lead_by, by) if half == 0 else (by, lead_by)))

    for place in (0, 1):
        for half in (0, 1):
            far = lax.rem(here[half] + 2, NX)
            for way in (0, 1):
                by = far_places[way][place]
                need_share(half, 2, by)
                tx1[half, way, by] = share(half, far, by).astype(jnp.bfloat16)
                first_copy(half, way, by).start()

    def ring_left():
        for kind in (KEY, VALUE, WEIGHT):
            sibling_copy(kind, 0, 0).wait_send()
            sibling_copy(kind, 0, 8).wait_send()
            for way in (0, 1):
                first_hop(kind, way).wait_send()
                if kind == WEIGHT or kind == way:
                    far_copy(kind, way).wait_send()

        def left(dist, _):
            for kind in (KEY, VALUE, WEIGHT):
                for way in (0, 1):
                    sibling_copy(kind, way, dist).wait_send()

                    @pl.when(dist < 7)
                    def _():
                        ring_copy(kind, way, dist).wait_send()

            return 0

        lax.fori_loop(1, 8, left, 0)

    def near(half, way):
        return lax.rem(here[half] + 1 + 2 * way, NX)

    for place in range(NX):
        for half in (0, 1):
            for way in (0, 1):
                by = near_order[way][place]
                need_share(half, 1 + 2 * way, by)
                term = share(half, near(half, way), by)
                if by in far_places[way]:
                    first_copy(half, way, by).wait_recv()
                    term = term + rx1[half, way, by].astype(jnp.float32)
                tx2[half, way, by] = term.astype(jnp.bfloat16)
                second_copy(half, way, by).start()
        if place == 0:
            for column in range(NX):
                for row in range(NX):
                    need(column, row)
            ring_left()
    for by in (2, 1, 3, 0):
        for half in (0, 1):
            for way in (0, 1):
                second_copy(half, way, by).wait_recv()
            total = (
                share(half, here[half], by)
                + rx2[half, 0, by].astype(jnp.float32)
                + rx2[half, 1, by].astype(jnp.float32)
            )
            if by:
                tx3[half, by - 1] = total.astype(jnp.bfloat16)
                third_copy(half, by).start()
            else:
                mid[half] = total

    for half in (0, 1):
        for way in (0, 1):
            for by in range(NX):
                if by in far_places[way]:
                    first_copy(half, way, by).wait_send()
                second_copy(half, way, by).wait_send()

    levels = gain_ref.shape[0]
    chosen = lax.broadcasted_iota(jnp.int32, (levels, 1), 0) == level_ref[0]
    gain_row = jnp.sum(jnp.where(chosen, gain_ref[...], 0.0), axis=0, keepdims=True)
    for half in (0, 1):
        total = mid[half]
        for by in (1, 3, 2):
            third_copy(half, by).wait_recv()
            total = total + rx3[half, by - 1].astype(jnp.float32)
        out_ref[half * HALF:(half + 1) * HALF, :] = (total * gain_row).astype(jnp.bfloat16)

    for half in (0, 1):
        for by in (1, 2, 3):
            third_copy(half, by).wait_send()


def on_device(query_rows, key_rows, value_rows, block_mask, noise_level, level_gain, out_weight):
    vmem = pl.BlockSpec(memory_space=pltpu.VMEM)
    hbm = pl.BlockSpec(memory_space=pltpu.HBM)
    smem = pl.BlockSpec(memory_space=pltpu.SMEM)
    dma = pltpu.SemaphoreType.DMA
    tokens = 2 * NZ * ROWS

    def b16(*shape):
        return pltpu.VMEM(shape, jnp.bfloat16)

    def f32(*shape):
        return pltpu.VMEM(shape, jnp.float32)

    return pl.pallas_call(
        kernel,
        out_shape=jax.ShapeDtypeStruct((ROWS, WIDTH), jnp.bfloat16),
        in_specs=[hbm, hbm, hbm, smem, smem, hbm, hbm],
        out_specs=vmem,
        scratch_shapes=[
            b16(ROWS, WIDTH), f32(*level_gain.shape),
            b16(tokens, WIDTH), b16(tokens, WIDTH), b16(NZ, 2, 192, WIDTH),
            f32(HEADS, ROWS, HD), f32(HEADS, ROWS, HD), f32(HEADS, ROWS, HD),
            b16(ROWS, WIDTH), f32(NX * NX, ROWS, WIDTH),
            b16(2, 2, 4, HALF, WIDTH), b16(2, 2, 4, HALF, WIDTH),
            b16(2, 2, 4, HALF, WIDTH), b16(2, 2, 4, HALF, WIDTH),
            b16(2, 3, HALF, WIDTH), b16(2, 3, HALF, WIDTH),
            f32(2, HALF, WIDTH),
            dma((3, 2, 8)), dma((3, 2, 9)), dma((3, 2, 9)), dma((3, 2, 9)),
            dma((2, 2, 4)), dma((2, 2, 4)), dma((2, 2, 4)), dma((2, 2, 4)), dma((2, 3)), dma((2, 3)),
            dma((5,)),
        ],
        compiler_params=pltpu.CompilerParams(
            collective_id=0, has_side_effects=True, vmem_limit_bytes=62 << 20
        ),
    )(query_rows, key_rows, value_rows, block_mask, noise_level, level_gain, out_weight.T)


def solution(mesh):
    return jax.shard_map(
        on_device,
        mesh=mesh,
        in_specs=(
            P("span", "head"),
            P("span", "head"),
            P("span", "head"),
            P("span", None),
            P("span"),
            P(None, "head"),
            P("head", "span"),
        ),
        out_specs=P("span", "head"),
        check_vma=False,
    )
```

```python
import functools
import math

import jax
import jax.numpy as jnp
from jax import lax
from jax.experimental import pallas as pl
from jax.experimental.pallas import tpu as pltpu
from jax.sharding import PartitionSpec as P

MESH = pl.DeviceIdType.MESH
HD = 128
NZ = 16
NX = 4
ROWS = 160
HALF = ROWS // 2
WIDTH = 384
HEADS = WIDTH // HD
NEG = -1e30
SCORE_SCALE = math.log2(math.e) / math.sqrt(HD)
KEY, VALUE, WEIGHT = 0, 1, 2


def kernel(
    q_hbm, k_hbm, v_hbm, mask_ref, level_ref, gain_hbm, w_hbm, out_ref,
    q_ref, gain_ref, kbuf, vbuf, wall, row_max, row_sum, acc, att, part,
    tx1, rx1, tx2, rx2, tx3, rx3, mid,
    ring_s, ring_r, sib_s, sib_r, s1, r1, s2, r2, s3, r3, load,
):
    span = lax.axis_index("span")
    group = lax.axis_index("head")
    z, core = span // 2, span % 2
    y, x = group // NX, group % NX
    z_up = (lax.rem(z + 1, NZ) * 2 + core, group)
    z_down = (lax.rem(z + NZ - 1, NZ) * 2 + core, group)
    sibling = (z * 2 + 1 - core, group)
    toward = [z_up, z_down]

    def in_plane(axis, by):
        if axis == 0:
            return (span, y * NX + lax.rem(x + by, NX))
        return (span, lax.rem(y + by, NX) * NX + x)

    own = [(k_hbm, kbuf.at[pl.ds(0, ROWS)]), (v_hbm, vbuf.at[pl.ds(0, ROWS)]),
           (w_hbm, wall.at[0, core]), (q_hbm, q_ref), (gain_hbm, gain_ref)]
    loads = [pltpu.make_async_copy(src, dst, load.at[i]) for i, (src, dst) in enumerate(own)]
    for copy in loads:
        copy.start()

    barrier = pltpu.get_barrier_semaphore()
    peers = [z_up, z_down, sibling] + [in_plane(a, b) for a in (0, 1) for b in (1, 2, 3)]
    for peer in peers:
        pl.semaphore_signal(barrier, inc=1, device_id=peer, device_id_type=MESH)
    pl.semaphore_wait(barrier, len(peers))

    def chunk_base(way, dist):
        return pl.multiple_of(320 + (dist - 1) * 640 + way * 320, 160)

    def chunk(kind, way, dist, own_ring=True):
        if kind == WEIGHT:
            slot = dist if isinstance(dist, int) and dist == 0 else dist + way * 8
            return wall.at[slot, core if own_ring else 1 - core]
        buf = kbuf if kind == KEY else vbuf
        sub = 0 if own_ring else 1
        if isinstance(dist, int) and dist == 0:
            return buf.at[pl.ds(sub * ROWS, ROWS)]
        return buf.at[pl.ds(pl.multiple_of(chunk_base(way, dist) + sub * ROWS, 160), ROWS)]

    def ring_copy(kind, way, dist):
        return pltpu.make_async_remote_copy(
            src_ref=chunk(kind, way, dist),
            dst_ref=chunk(kind, way, dist + 1),
            send_sem=ring_s.at[kind, way, dist],
            recv_sem=ring_r.at[kind, way, dist + 1],
            device_id=toward[way],
            device_id_type=MESH,
        )

    def first_hop(kind, way):
        return pltpu.make_async_remote_copy(
            src_ref=own[kind][0],
            dst_ref=chunk(kind, way, 1),
            send_sem=ring_s.at[kind, way, 0],
            recv_sem=ring_r.at[kind, way, 1],
            device_id=toward[way],
            device_id_type=MESH,
        )

    def far_copy(kind, way):
        src, dst = chunk(kind, way, 7), chunk(kind, 0, 8)
        if kind == WEIGHT:
            src, dst = src.at[pl.ds(way * 96, 96)], dst.at[pl.ds(way * 96, 96)]
        return pltpu.make_async_remote_copy(
            src_ref=src,
            dst_ref=dst,
            send_sem=ring_s.at[kind, way, 7],
            recv_sem=ring_r.at[kind, way, 8],
            device_id=toward[way],
            device_id_type=MESH,
        )

    def arrival(kind, way, dist):
        landed = chunk(kind, way, dist)
        return pltpu.make_async_remote_copy(
            src_ref=landed,
            dst_ref=landed,
            send_sem=ring_s.at[kind, way, dist - 1],
            recv_sem=ring_r.at[kind, way, dist],
            device_id=toward[way],
            device_id_type=MESH,
        )

    def sibling_copy(kind, way, dist):
        dst = chunk(kind, way, dist, kind == WEIGHT)
        return pltpu.make_async_remote_copy(
            src_ref=chunk(kind, way, dist),
            dst_ref=dst,
            send_sem=sib_s.at[kind, way, dist],
            recv_sem=sib_r.at[kind, way, dist],
            device_id=sibling,
            device_id_type=MESH,
        )

    def sibling_arrival(kind, way, dist):
        landed = chunk(kind, way, dist, False)
        return pltpu.make_async_remote_copy(
            src_ref=landed,
            dst_ref=landed,
            send_sem=sib_s.at[kind, way, dist],
            recv_sem=sib_r.at[kind, way, dist],
            device_id=sibling,
            device_id_type=MESH,
        )

    for kind in (KEY, VALUE, WEIGHT):
        for way in (0, 1):
            first_hop(kind, way).start()
    for kind in (KEY, VALUE, WEIGHT):
        loads[kind].wait()
        sibling_copy(kind, 0, 0).start()
    loads[3].wait()
    loads[4].wait()

    row_max[...] = jnp.full_like(row_max, NEG)
    row_sum[...] = jnp.zeros_like(row_sum)
    acc[...] = jnp.zeros_like(acc)

    def visible(chip, which):
        return mask_ref[0, lax.rem(chip + 2 * NZ, NZ) * 2 + which]

    def attend(base, seen):
        count = len(seen) * ROWS
        lane_span = lax.broadcasted_iota(jnp.int32, (1, count), 1) // ROWS
        bias = jnp.zeros((1, count), jnp.float32)
        for place, flag in enumerate(seen):
            bias = jnp.where(lane_span == place, jnp.where(flag > 0, 0.0, NEG), bias)
        for head in range(HEADS):
            cols = slice(head * HD, (head + 1) * HD)
            scores = lax.dot_general(
                q_ref[:, cols], kbuf[pl.ds(base, count), cols], (((1,), (1,)), ((), ())),
                preferred_element_type=jnp.float32,
            )
            scores = scores * SCORE_SCALE + bias
            old_max = row_max[head][:, 0:1]
            new_max = jnp.maximum(old_max, jnp.max(scores, axis=1, keepdims=True))
            probs = jnp.exp2(scores - new_max)
            factor = jnp.exp2(old_max - new_max)
            total = row_sum[head][:, 0:1] * factor + jnp.sum(probs, axis=1, keepdims=True)
            row_max[head] = jnp.broadcast_to(new_max, (ROWS, HD))
            row_sum[head] = jnp.broadcast_to(total, (ROWS, HD))
            acc[head] = acc[head] * factor + jnp.dot(
                probs.astype(jnp.bfloat16), vbuf[pl.ds(base, count), cols],
                preferred_element_type=jnp.float32,
            )

    sibling_arrival(KEY, 0, 0).wait_recv()
    sibling_arrival(VALUE, 0, 0).wait_recv()
    attend(0, [visible(z, core), visible(z, 1 - core)])

    def hop(dist, _):
        for kind in (KEY, VALUE):
            for way in (0, 1):
                arrival(kind, way, dist).wait_recv()

                @pl.when(dist < 7)
                def _():
                    ring_copy(kind, way, dist).start()

                if kind != WEIGHT:
                    send_far = way == kind

                    @pl.when(dist == 7)
                    def _():
                        if send_far:
                            far_copy(kind, way).start()
                else:

                    @pl.when(dist == 7)
                    def _():
                        far_copy(kind, way).start()

                sibling_copy(kind, way, dist).start()
        for kind in (KEY, VALUE):
            for way in (0, 1):
                sibling_arrival(kind, way, dist).wait_recv()
        attend(
            chunk_base(0, dist),
            [
                visible(z - dist, core), visible(z - dist, 1 - core),
                visible(z + dist, core), visible(z + dist, 1 - core),
            ],
        )
        for kind in (WEIGHT,):
            for way in (0, 1):
                arrival(kind, way, dist).wait_recv()

                @pl.when(dist < 7)
                def _():
                    ring_copy(kind, way, dist).start()

                if kind != WEIGHT:
                    send_far = way == kind

                    @pl.when(dist == 7)
                    def _():
                        if send_far:
                            far_copy(kind, way).start()
                else:

                    @pl.when(dist == 7)
                    def _():
                        far_copy(kind, way).start()

                sibling_copy(kind, way, dist).start()
        return 0

    for dist in range(1, 8):
        hop(dist, 0)

    far_copy(KEY, 0).wait_recv()
    sibling_copy(KEY, 0, 8).start()
    far_copy(VALUE, 1).wait_recv()
    sibling_copy(VALUE, 0, 8).start()
    sibling_arrival(KEY, 0, 8).wait_recv()
    sibling_arrival(VALUE, 0, 8).wait_recv()
    attend(chunk_base(0, 8), [visible(z - 8, core), visible(z - 8, 1 - core)])
    for head in range(HEADS):
        per_row = 1.0 / row_sum[head][:, 0:1]
        att[:, head * HD:(head + 1) * HD] = (acc[head] * per_row).astype(jnp.bfloat16)

    for way in (0, 1):
        far_copy(WEIGHT, way).wait_recv()
    sibling_copy(WEIGHT, 0, 8).start()
    sibling_arrival(WEIGHT, 0, 0).wait_recv()

    def weights_in(dist, _):
        for way in (0, 1):
            sibling_arrival(WEIGHT, way, dist).wait_recv()
        return 0

    lax.fori_loop(1, 8, weights_in, 0)
    sibling_arrival(WEIGHT, 0, 8).wait_recv()

    def project(column, row):
        block = row * NX + column
        away = lax.rem(z - block + NZ, NZ)
        slot = jnp.where(away <= 8, away, 24 - away)
        part[block] = lax.dot_general(
            att[...], wall[slot].reshape(WIDTH, WIDTH), (((1,), (1,)), ((), ())),
            preferred_element_type=jnp.float32,
        )

    here = [x, y]

    def block_at(half, lead, other):
        return other * NX + lead if half == 0 else lead * NX + other

    def share(half, lead, by):
        other = lax.rem(here[1 - half] + by, NX)
        return part[block_at(half, lead, other), half * HALF:(half + 1) * HALF, :]

    def send(src, dst, ssem, rsem, axis, by):
        return pltpu.make_async_remote_copy(
            src_ref=src, dst_ref=dst, send_sem=ssem, recv_sem=rsem,
            device_id=in_plane(axis, by), device_id_type=MESH,
        )

    def first_copy(half, way, by):
        at = (half, way, by)
        return send(tx1.at[at], rx1.at[at], s1.at[at], r1.at[at], half, 1 + 2 * way)

    def second_copy(half, way, by):
        at = (half, way, by)
        return send(tx2.at[at], rx2.at[at], s2.at[at], r2.at[at], half, 1 + 2 * way)

    def third_copy(half, by):
        at = (half, by - 1)
        return send(tx3.at[at], rx3.at[at], s3.at[at], r3.at[at], 1 - half, by)

    far_places = ((1, 0), (2, 3))
    near_order = ((2, 1, 3, 0), (1, 2, 3, 0))
    projected = set()

    def need(column, row):
        if (column, row) not in projected:
            projected.add((column, row))
            project(lax.rem(x + column, NX), lax.rem(y + row, NX))

    def need_share(half, lead_by, by):
        need(*((lead_by, by) if half == 0 else (by, lead_by)))

    for place in (0, 1):
        for half in (0, 1):
            far = lax.rem(here[half] + 2, NX)
            for way in (0, 1):
                by = far_places[way][place]
                need_share(half, 2, by)
                tx1[half, way, by] = share(half, far, by).astype(jnp.bfloat16)
                first_copy(half, way, by).start()

    def ring_left():
        for kind in (KEY, VALUE, WEIGHT):
            sibling_copy(kind, 0, 0).wait_send()
            sibling_copy(kind, 0, 8).wait_send()
            for way in (0, 1):
                first_hop(kind, way).wait_send()
                if kind == WEIGHT or kind == way:
                    far_copy(kind, way).wait_send()

        def left(dist, _):
            for kind in (KEY, VALUE, WEIGHT):
                for way in (0, 1):
                    sibling_copy(kind, way, dist).wait_send()

                    @pl.when(dist < 7)
                    def _():
                        ring_copy(kind, way, dist).wait_send()

            return 0

        lax.fori_loop(1, 8, left, 0)

    def near(half, way):
        return lax.rem(here[half] + 1 + 2 * way, NX)

    for place in range(NX):
        for half in (0, 1):
            for way in (0, 1):
                by = near_order[way][place]
                need_share(half, 1 + 2 * way, by)
                term = share(half, near(half, way), by)
                if by in far_places[way]:
                    first_copy(half, way, by).wait_recv()
                    term = term + rx1[half, way, by].astype(jnp.float32)
                tx2[half, way, by] = term.astype(jnp.bfloat16)
                second_copy(half, way, by).start()
        if place == 0:
            for column in range(NX):
                for row in range(NX):
                    need(column, row)
            ring_left()
    for by in (2, 1, 3, 0):
        for half in (0, 1):
            for way in (0, 1):
                second_copy(half, way, by).wait_recv()
            total = (
                share(half, here[half], by)
                + rx2[half, 0, by].astype(jnp.float32)
                + rx2[half, 1, by].astype(jnp.float32)
            )
            if by:
                tx3[half, by - 1] = total.astype(jnp.bfloat16)
                third_copy(half, by).start()
            else:
                mid[half] = total

    for half in (0, 1):
        for way in (0, 1):
            for by in range(NX):
                if by in far_places[way]:
                    first_copy(half, way, by).wait_send()
                second_copy(half, way, by).wait_send()

    levels = gain_ref.shape[0]
    chosen = lax.broadcasted_iota(jnp.int32, (levels, 1), 0) == level_ref[0]
    gain_row = jnp.sum(jnp.where(chosen, gain_ref[...], 0.0), axis=0, keepdims=True)
    for half in (0, 1):
        total = mid[half]
        for by in (1, 3, 2):
            third_copy(half, by).wait_recv()
            total = total + rx3[half, by - 1].astype(jnp.float32)
        out_ref[half * HALF:(half + 1) * HALF, :] = (total * gain_row).astype(jnp.bfloat16)

    for half in (0, 1):
        for by in (1, 2, 3):
            third_copy(half, by).wait_send()


def on_device(query_rows, key_rows, value_rows, block_mask, noise_level, level_gain, out_weight):
    vmem = pl.BlockSpec(memory_space=pltpu.VMEM)
    hbm = pl.BlockSpec(memory_space=pltpu.HBM)
    smem = pl.BlockSpec(memory_space=pltpu.SMEM)
    dma = pltpu.SemaphoreType.DMA
    tokens = 2 * NZ * ROWS

    def b16(*shape):
        return pltpu.VMEM(shape, jnp.bfloat16)

    def f32(*shape):
        return pltpu.VMEM(shape, jnp.float32)

    return pl.pallas_call(
        kernel,
        out_shape=jax.ShapeDtypeStruct((ROWS, WIDTH), jnp.bfloat16),
        in_specs=[hbm, hbm, hbm, smem, smem, hbm, hbm],
        out_specs=vmem,
        scratch_shapes=[
            b16(ROWS, WIDTH), f32(*level_gain.shape),
            b16(tokens, WIDTH), b16(tokens, WIDTH), b16(NZ, 2, 192, WIDTH),
            f32(HEADS, ROWS, HD), f32(HEADS, ROWS, HD), f32(HEADS, ROWS, HD),
            b16(ROWS, WIDTH), f32(NX * NX, ROWS, WIDTH),
            b16(2, 2, 4, HALF, WIDTH), b16(2, 2, 4, HALF, WIDTH),
            b16(2, 2, 4, HALF, WIDTH), b16(2, 2, 4, HALF, WIDTH),
            b16(2, 3, HALF, WIDTH), b16(2, 3, HALF, WIDTH),
            f32(2, HALF, WIDTH),
            dma((3, 2, 8)), dma((3, 2, 9)), dma((3, 2, 9)), dma((3, 2, 9)),
            dma((2, 2, 4)), dma((2, 2, 4)), dma((2, 2, 4)), dma((2, 2, 4)), dma((2, 3)), dma((2, 3)),
            dma((5,)),
        ],
        compiler_params=pltpu.CompilerParams(
            collective_id=0, has_side_effects=True, vmem_limit_bytes=62 << 20
        ),
    )(query_rows, key_rows, value_rows, block_mask, noise_level, level_gain, out_weight.T)


def solution(mesh):
    return jax.shard_map(
        on_device,
        mesh=mesh,
        in_specs=(
            P("span", "head"),
            P("span", "head"),
            P("span", "head"),
            P("span", None),
            P("span"),
            P(None, "head"),
            P("head", "span"),
        ),
        out_specs=P("span", "head"),
        check_vma=False,
    )
```
